32 devices in a mesh: sta: 16 (over z, x, core), band: 2 (over y).
Axes of the slice: x: 2, y: 2, z: 4, core: 2. Of those that a mesh axis runs over, the one named last changes fastest.
Arguments:
- spectra: bfloat16 [2, 8, 6144, 1024], P(None, None, 'sta', 'band')
- half_width: int32 [1024], P('band'), may hold values from 1 to 8, as said below
Outputs:
- correlations: bfloat16 [6144, 3, 8, 384], P('sta', None, 'band')
The draws below stay inside these ranges and needn't reach their ends.
Inputs may be any that keep to these rules, and one draw needn't show every extreme that they name: `half_width`: at most 8, and exactly 8 at one bin or more.
All inputs are finite; a program needn't handle non-finite values.
Results may differ from the reference program's by a relative error of at most 0.0062.
Values may be sent and summed in bfloat16 or wider, within the bound.
A program may use at most 192 MiB of HBM per device.

```python
import math
import jax
import jax.numpy as jnp
from jax import lax

GRP_ST = 128
NF = 1024
SEGS = 8
ROUNDS = 3
LAGS = 4
LAG_STEP = 8
WMAX = 8
CHANNELS = 6144
N_STA = 16
N_BAND = 2


def draw_spectra(key, part):
    shape = (2, SEGS, CHANNELS, NF)
    first, second, third, fourth = jax.random.split(key, 4)
    base = jax.random.normal(first, shape, jnp.float32)
    chan_scale = jnp.exp(jax.random.uniform(second, (1, 1, CHANNELS, 1), jnp.float32, -1.15, 1.15))
    bin_scale = jnp.exp(jax.random.uniform(third, (1, 1, 1, NF), jnp.float32, -1.15, 1.15))
    rough_scale = jnp.exp(jax.random.uniform(fourth, (1, 1, CHANNELS, NF), jnp.float32, -0.7, 0.7))
    return (base * chan_scale * bin_scale * rough_scale).astype(jnp.bfloat16)


def draw_half_width(key, part):
    widths = jax.random.randint(key, (NF,), 1, WMAX + 1, jnp.int32)
    where_most = jax.random.randint(jax.random.fold_in(key, 1), (), 0, NF, jnp.int32)
    return widths.at[where_most].set(WMAX)


def setup_inputs(seed: int = 0) -> dict:
    arg_keys = jax.random.split(jax.random.key(seed), 3)
    return {
        "spectra": draw_spectra(jax.random.fold_in(arg_keys[2], 71), 0),
        "half_width": draw_half_width(jax.random.fold_in(arg_keys[2], 71), 0),
    }


def rotate_part(part, cosines, sines):
    real_part = part[0].astype(jnp.float32)[None]
    imag_part = part[1].astype(jnp.float32)[None]
    cos_block = cosines[:, None, None, :]
    sin_block = sines[:, None, None, :]
    rot_real = (real_part * cos_block - imag_part * sin_block).astype(jnp.bfloat16)
    rot_imag = (real_part * sin_block + imag_part * cos_block).astype(jnp.bfloat16)
    return jnp.stack([rot_real, rot_imag])

def reference(spectra, half_width):
    stations = GRP_ST * N_STA
    group_chans = 3 * GRP_ST
    band_bins = NF // N_BAND
    energy = lax.optimization_barrier(jnp.sum(jnp.square(spectra.astype(jnp.float32)), axis=(0, 1)))
    energy = lax.optimization_barrier(jnp.sum(energy.reshape(stations, 3, NF), axis=1))
    positions = jnp.arange(NF, dtype=jnp.int32)
    distance = jnp.abs(positions[:, None] - positions[None, :])
    window = (distance <= half_width[None, :]).astype(jnp.float32)
    window_sum = jnp.dot(energy, window, precision=lax.Precision.HIGHEST)
    counts = lax.optimization_barrier(jnp.sum(window, axis=0))
    amplitude = jnp.sqrt(window_sum / (3.0 * SEGS * counts) + 1e-06)
    whitened = (spectra.astype(jnp.float32) / jnp.repeat(amplitude, 3, axis=0)[None, None]).astype(jnp.bfloat16)
    groups = jnp.transpose(whitened.reshape(2, SEGS, N_STA, group_chans, NF), (2, 0, 1, 3, 4))
    lag_values = jnp.arange(LAGS, dtype=jnp.float32) * LAG_STEP
    phases = math.pi * lag_values[:, None] * positions.astype(jnp.float32)[None, :] / NF
    cosines = jnp.cos(phases)
    sines = jnp.sin(phases)
    norm_factor = 1.0 / math.sqrt(SEGS * band_bins)

    def one_group(group_index):
        own_part = lax.dynamic_index_in_dim(groups, group_index, 0, keepdims=False)
        left_side = own_part.astype(jnp.float32).reshape(2, SEGS, group_chans, N_BAND, band_bins)
        results = []
        for offset in range(1, ROUNDS + 1):
            partner_index = ((group_index - offset) % N_STA).astype(jnp.int32)
            partner = lax.dynamic_index_in_dim(groups, partner_index, 0, keepdims=False)
            rotated = rotate_part(partner, cosines, sines)
            right_side = rotated.astype(jnp.float32).reshape(2, LAGS, SEGS, group_chans, N_BAND, band_bins)
            summed = jnp.einsum('cspbf,clsqbf->pblq', left_side, right_side, precision=lax.Precision.HIGHEST) * norm_factor
            results.append(summed.reshape(group_chans, N_BAND * LAGS, group_chans).astype(jnp.bfloat16))
        return jnp.stack(results, axis=1)
    stacked = lax.map(one_group, jnp.arange(N_STA, dtype=jnp.int32))
    return stacked.reshape(stations * 3, ROUNDS, N_BAND * LAGS, group_chans)
```

```python
import functools
import math

import jax
import jax.numpy as jnp
from jax import lax
from jax.experimental import pallas as pl
from jax.experimental.pallas import tpu as pltpu
from jax.sharding import PartitionSpec as P

ROUNDS = 3
LAGS = 4
LAG_STEP = 8
WMAX = 8
LANES = 128
ROWS = 32
EARLY = 2
MESH = pl.DeviceIdType.MESH
HIGHEST = lax.Precision.HIGHEST
F32 = jnp.float32
BF16 = jnp.bfloat16


def kernel(
    groups, bands, spectra, half_width, cosines, sines, out,
    rot, got, acc, amps, scale, energy, padded,
    load_sem, send_sem, recv_sem, edge_send, edge_recv,
):
    _, segs, chans, bins = spectra.shape
    stations = chans // 3
    me = lax.axis_index("sta")
    band = lax.axis_index("band")
    core = lax.rem(me, 2)
    odd = lax.rem(me // 2, 2)
    first = core == 0
    second = core == 1
    direct = jnp.logical_or(odd == 0, first)
    relays = jnp.logical_and(odd == 1, first)

    def at(step):
        return {"sta": lax.rem(me + step + groups, groups)}

    right = {"band": lax.rem(band + 1, bands)}
    left = {"band": lax.rem(band + bands - 1, bands)}

    barrier = pltpu.get_barrier_semaphore()
    peers = [at(step) for step in (-3, -2, -1, 1, 2, 3)] + [left, right]
    for peer in peers:
        pl.semaphore_signal(barrier, inc=1, device_id=peer, device_id_type=MESH)
    pl.semaphore_wait(barrier, len(peers))

    def copy(flow, slot, step, s, source):
        last = isinstance(s, int) and s == segs
        target = amps.at[slot] if last else got.at[slot, s]
        if source is None:
            origin = amps.at[ROUNDS] if last else spectra.at[:, s]
        else:
            origin = amps.at[source] if last else got.at[source, s]
        return pltpu.make_async_remote_copy(
            src_ref=origin, dst_ref=target,
            send_sem=send_sem.at[flow, s], recv_sem=recv_sem.at[slot, s],
            device_id=at(step), device_id_type=MESH,
        )

    own_flows = [
        (direct, lambda s: copy(0, 1, 2, s, None)),
        (second, lambda s: copy(1, 2, 3, s, None)),
        (first, lambda s: copy(2, 0, 1, s, None)),
    ]
    relay = (relays, lambda s: copy(3, 1, -1, s, 2))
    swaps = [
        (first, lambda s: copy(4, 2, 1, s, 1)),
        (second, lambda s: copy(4, 0, -1, s, 1)),
    ]

    def start(flows, s):
        for cond, make in flows:
            @pl.when(cond)
            def _():
                make(s).start()

    def arrived(slot, s):
        copy(0, slot, 2, s, None).wait_recv()

    def forward(s):
        @pl.when(relays)
        def _():
            arrived(2, s)
            relay[1](s).start()

    def arrived_third(s):
        @pl.when(jnp.logical_not(relays))
        def _():
            arrived(2, s)

    def load(s):
        return pltpu.make_async_copy(spectra.at[:, s], rot.at[s, :, 0], load_sem.at[s])

    @pl.loop(0, segs)
    def _(s):
        load(s).start()

    @pl.loop(0, EARLY)
    def _(s):
        start(own_flows, s)

    @pl.loop(0, segs)
    def _(s):
        load(s).wait()

    @pl.loop(0, chans // ROWS)
    def _(i):
        rows = pl.ds(pl.multiple_of(i * ROWS, ROWS), ROWS)
        total = jnp.zeros((ROWS, bins), F32)
        for s in range(segs):
            for c in range(2):
                part = rot[s, c, 0, rows, :].astype(F32)
                total = total + part * part
        energy[rows, :] = total

    member = (
        lax.broadcasted_iota(jnp.int32, (stations, chans), 1) // 3
        == lax.broadcasted_iota(jnp.int32, (stations, chans), 0)
    ).astype(F32)
    spread = (
        lax.broadcasted_iota(jnp.int32, (chans, stations), 0) // 3
        == lax.broadcasted_iota(jnp.int32, (chans, stations), 1)
    ).astype(F32)
    padded[:, LANES:LANES + bins] = jnp.dot(
        member, energy[...], precision=HIGHEST, preferred_element_type=F32
    )
    to_right = pltpu.make_async_remote_copy(
        src_ref=padded.at[:, pl.ds(bins, LANES)], dst_ref=padded.at[:, pl.ds(0, LANES)],
        send_sem=edge_send.at[0], recv_sem=edge_recv.at[0],
        device_id=right, device_id_type=MESH,
    )
    to_left = pltpu.make_async_remote_copy(
        src_ref=padded.at[:, pl.ds(LANES, LANES)],
        dst_ref=padded.at[:, pl.ds(LANES + bins, LANES)],
        send_sem=edge_send.at[1], recv_sem=edge_recv.at[1],
        device_id=left, device_id_type=MESH,
    )
    to_right.start()
    to_left.start()
    to_right.wait()
    to_left.wait()

    width = half_width[...]
    place = band * bins + lax.broadcasted_iota(jnp.int32, (1, bins), 1)
    window_sum = jnp.zeros((stations, bins), F32)
    counts = jnp.zeros((1, bins), F32)
    for d in range(-WMAX, WMAX + 1):
        other = place + d
        inside = (abs(d) <= width) & (other >= 0) & (other < bands * bins)
        weight = inside.astype(F32)
        window_sum = window_sum + jnp.where(
            jnp.broadcast_to(weight, (stations, bins)) > 0.0,
            padded[:, LANES + d:LANES + d + bins], 0.0,
        )
        counts = counts + weight
    amps[ROUNDS] = 1.0 / jnp.sqrt(window_sum / (3.0 * segs * counts) + 1e-06)

    start(own_flows, segs)

    @pl.loop(EARLY, segs)
    def _(s):
        start(own_flows, s)

    def expand(slot):
        scale[slot] = jnp.dot(
            spread, amps[slot], precision=HIGHEST, preferred_element_type=F32
        )

    expand(ROUNDS)

    @pl.loop(0, segs)
    def _(s):
        @pl.loop(0, chans // ROWS)
        def _(i):
            rows = pl.ds(pl.multiple_of(i * ROWS, ROWS), ROWS)
            factor = scale[ROUNDS, rows, :]
            real = (rot[s, 0, 0, rows, :].astype(F32) * factor).astype(BF16)
            imag = (rot[s, 1, 0, rows, :].astype(F32) * factor).astype(BF16)
            rot[s, 0, 0, rows, :] = real
            rot[s, 1, 0, rows, :] = imag
            real = real.astype(F32)
            imag = imag.astype(F32)
            for lag in range(1, LAGS):
                cosine = cosines[lag:lag + 1, :]
                sine = sines[lag:lag + 1, :]
                rot[s, 0, lag, rows, :] = (real * cosine + imag * sine).astype(BF16)
                rot[s, 1, lag, rows, :] = (imag * cosine - real * sine).astype(BF16)

    forward(segs)
    forward(0)
    arrived(1, segs)
    start(swaps, segs)
    acc[...] = jnp.zeros_like(acc)
    expand(1)
    arrived_third(segs)
    expand(2)
    arrived(0, segs)
    expand(0)

    def add(slot, s):
        for c in range(2):
            other = (got[slot, s, c].astype(F32) * scale[slot]).astype(BF16)
            mine = rot[s, c].reshape(LAGS * chans, bins)
            acc[slot] += lax.dot_general(
                mine, other, (((1,), (1,)), ((), ())), preferred_element_type=F32
            )

    @pl.loop(0, segs)
    def _(s):
        @pl.when(s + 1 < segs)
        def _():
            forward(s + 1)

        arrived(1, s)
        start(swaps, s)
        add(1, s)
        arrived_third(s)
        add(2, s)
        arrived(0, s)
        add(0, s)

    norm = 1.0 / math.sqrt(segs * bins)
    for slot in range(ROUNDS):
        @pl.loop(0, LAGS * chans // ROWS)
        def _(i):
            rows = pl.ds(pl.multiple_of(i * ROWS, ROWS), ROWS)
            out[slot, rows, :] = (acc[slot, rows, :] * norm).astype(BF16)

    def sent(s):
        for cond, make in own_flows + [relay] + swaps:
            @pl.when(cond)
            def _():
                make(s).wait_send()

    @pl.loop(0, segs)
    def _(s):
        sent(s)

    sent(segs)


def shards(groups, bands, spectra, half_width):
    _, segs, chans, bins = spectra.shape
    inner = lax.axis_index("band") * bins + jnp.arange(bins, dtype=jnp.int32)
    lag_values = jnp.arange(LAGS, dtype=F32) * LAG_STEP
    phases = math.pi * lag_values[:, None] * inner.astype(F32)[None, :] / (bands * bins)
    vmem = pl.BlockSpec(memory_space=pltpu.VMEM)
    pieces = segs + 1
    out = pl.pallas_call(
        functools.partial(kernel, groups, bands),
        out_shape=jax.ShapeDtypeStruct((ROUNDS, LAGS * chans, chans), BF16),
        in_specs=[pl.BlockSpec(memory_space=pl.ANY), vmem, vmem, vmem],
        out_specs=vmem,
        scratch_shapes=[
            pltpu.VMEM((segs, 2, LAGS, chans, bins), BF16),
            pltpu.VMEM((ROUNDS, segs, 2, chans, bins), BF16),
            pltpu.VMEM((ROUNDS, LAGS * chans, chans), F32),
            pltpu.VMEM((ROUNDS + 1, chans // 3, bins), F32),
            pltpu.VMEM((ROUNDS + 1, chans, bins), F32),
            pltpu.VMEM((chans, bins), F32),
            pltpu.VMEM((chans // 3, bins + 2 * LANES), F32),
            pltpu.SemaphoreType.DMA((segs,)),
            pltpu.SemaphoreType.DMA((5, pieces)),
            pltpu.SemaphoreType.DMA((ROUNDS, pieces)),
            pltpu.SemaphoreType.DMA((2,)),
            pltpu.SemaphoreType.DMA((2,)),
        ],
        compiler_params=pltpu.CompilerParams(
            collective_id=0, has_side_effects=True, vmem_limit_bytes=66_500_000
        ),
        cost_estimate=pl.CostEstimate(
            flops=2 * ROUNDS * LAGS * chans * chans * 2 * segs * bins,
            bytes_accessed=2 * spectra.size * 4, transcendentals=0,
        ),
    )(spectra, half_width.reshape(1, bins), jnp.cos(phases), jnp.sin(phases))
    return jnp.transpose(out.reshape(ROUNDS, LAGS, chans, chans), (2, 0, 1, 3))


def solution(mesh):
    in_specs = (P(None, None, "sta", "band"), P("band"))
    out_specs = P("sta", None, "band", None)
    body = functools.partial(shards, mesh.shape["sta"], mesh.shape["band"])
    return jax.shard_map(body, mesh=mesh, in_specs=in_specs, out_specs=out_specs, check_vma=False)
```

```python
import functools
import math

import jax
import jax.numpy as jnp
from jax import lax
from jax.experimental import pallas as pl
from jax.experimental.pallas import tpu as pltpu
from jax.sharding import PartitionSpec as P

ROUNDS = 3
LAGS = 4
LAG_STEP = 8
WMAX = 8
LANES = 128
ROWS = 32
EARLY = 2
MESH = pl.DeviceIdType.MESH
HIGHEST = lax.Precision.HIGHEST
F32 = jnp.float32
BF16 = jnp.bfloat16


def kernel(
    groups, bands, spectra, half_width, cosines, sines, out,
    rot, got, acc, amps, scale, energy, padded,
    load_sem, send_sem, recv_sem, edge_send, edge_recv,
):
    _, segs, chans, bins = spectra.shape
    stations = chans // 3
    me = lax.axis_index("sta")
    band = lax.axis_index("band")
    core = lax.rem(me, 2)
    odd = lax.rem(me // 2, 2)
    first = core == 0
    second = core == 1
    direct = jnp.logical_or(odd == 0, first)
    relays = jnp.logical_and(odd == 1, first)

    def at(step):
        return {"sta": lax.rem(me + step + groups, groups)}

    right = {"band": lax.rem(band + 1, bands)}
    left = {"band": lax.rem(band + bands - 1, bands)}

    barrier = pltpu.get_barrier_semaphore()
    peers = [at(step) for step in (-3, -2, -1, 1, 2, 3)] + [left, right]
    for peer in peers:
        pl.semaphore_signal(barrier, inc=1, device_id=peer, device_id_type=MESH)
    pl.semaphore_wait(barrier, len(peers))

    def copy(flow, slot, step, s, source):
        last = isinstance(s, int) and s == segs
        target = amps.at[slot] if last else got.at[slot, s]
        if source is None:
            origin = amps.at[ROUNDS] if last else spectra.at[:, s]
        else:
            origin = amps.at[source] if last else got.at[source, s]
        return pltpu.make_async_remote_copy(
            src_ref=origin, dst_ref=target,
            send_sem=send_sem.at[flow, s], recv_sem=recv_sem.at[slot, s],
            device_id=at(step), device_id_type=MESH,
        )

    own_flows = [
        (direct, lambda s: copy(0, 1, 2, s, None)),
        (second, lambda s: copy(1, 2, 3, s, None)),
        (first, lambda s: copy(2, 0, 1, s, None)),
    ]
    relay = (relays, lambda s: copy(3, 1, -1, s, 2))
    swaps = [
        (first, lambda s: copy(4, 2, 1, s, 1)),
        (second, lambda s: copy(4, 0, -1, s, 1)),
    ]

    def start(flows, s):
        for cond, make in flows:
            @pl.when(cond)
            def _():
                make(s).start()

    def arrived(slot, s):
        copy(0, slot, 2, s, None).wait_recv()

    def forward(s):
        @pl.when(relays)
        def _():
            arrived(2, s)
            relay[1](s).start()

    def arrived_third(s):
        @pl.when(jnp.logical_not(relays))
        def _():
            arrived(2, s)

    def load(s):
        return pltpu.make_async_copy(spectra.at[:, s], rot.at[s, :, 0], load_sem.at[s])

    @pl.loop(0, segs)
    def _(s):
        load(s).start()

    start(own_flows, 0)

    @pl.loop(0, segs)
    def _(s):
        load(s).wait()

    @pl.loop(0, chans // ROWS)
    def _(i):
        rows = pl.ds(pl.multiple_of(i * ROWS, ROWS), ROWS)
        total = jnp.zeros((ROWS, bins), F32)
        for s in range(segs):
            for c in range(2):
                part = rot[s, c, 0, rows, :].astype(F32)
                total = total + part * part
        energy[rows, :] = total

    @pl.loop(1, EARLY)
    def _(s):
        start(own_flows, s)

    member = (
        lax.broadcasted_iota(jnp.int32, (stations, chans), 1) // 3
        == lax.broadcasted_iota(jnp.int32, (stations, chans), 0)
    ).astype(F32)
    spread = (
        lax.broadcasted_iota(jnp.int32, (chans, stations), 0) // 3
        == lax.broadcasted_iota(jnp.int32, (chans, stations), 1)
    ).astype(F32)
    padded[:, LANES:LANES + bins] = jnp.dot(
        member, energy[...], precision=HIGHEST, preferred_element_type=F32
    )
    to_right = pltpu.make_async_remote_copy(
        src_ref=padded.at[:, pl.ds(bins, LANES)], dst_ref=padded.at[:, pl.ds(0, LANES)],
        send_sem=edge_send.at[0], recv_sem=edge_recv.at[0],
        device_id=right, device_id_type=MESH,
    )
    to_left = pltpu.make_async_remote_copy(
        src_ref=padded.at[:, pl.ds(LANES, LANES)],
        dst_ref=padded.at[:, pl.ds(LANES + bins, LANES)],
        send_sem=edge_send.at[1], recv_sem=edge_recv.at[1],
        device_id=left, device_id_type=MESH,
    )
    to_right.start()
    to_left.start()
    to_right.wait()
    to_left.wait()

    width = half_width[...]
    place = band * bins + lax.broadcasted_iota(jnp.int32, (1, bins), 1)
    window_sum = jnp.zeros((stations, bins), F32)
    counts = jnp.zeros((1, bins), F32)
    for d in range(-WMAX, WMAX + 1):
        other = place + d
        inside = (abs(d) <= width) & (other >= 0) & (other < bands * bins)
        weight = inside.astype(F32)
        window_sum = window_sum + jnp.where(
            jnp.broadcast_to(weight, (stations, bins)) > 0.0,
            padded[:, LANES + d:LANES + d + bins], 0.0,
        )
        counts = counts + weight
    amps[ROUNDS] = 1.0 / jnp.sqrt(window_sum / (3.0 * segs * counts) + 1e-06)

    start(own_flows, segs)

    @pl.loop(EARLY, segs)
    def _(s):
        start(own_flows, s)

    forward(0)

    def expand(slot):
        scale[slot] = jnp.dot(
            spread, amps[slot], precision=HIGHEST, preferred_element_type=F32
        )

    expand(ROUNDS)

    @pl.loop(0, segs)
    def _(s):
        @pl.loop(0, chans // ROWS)
        def _(i):
            rows = pl.ds(pl.multiple_of(i * ROWS, ROWS), ROWS)
            factor = scale[ROUNDS, rows, :]
            real = (rot[s, 0, 0, rows, :].astype(F32) * factor).astype(BF16)
            imag = (rot[s, 1, 0, rows, :].astype(F32) * factor).astype(BF16)
            rot[s, 0, 0, rows, :] = real
            rot[s, 1, 0, rows, :] = imag
            real = real.astype(F32)
            imag = imag.astype(F32)
            for lag in range(1, LAGS):
                cosine = cosines[lag:lag + 1, :]
                sine = sines[lag:lag + 1, :]
                rot[s, 0, lag, rows, :] = (real * cosine + imag * sine).astype(BF16)
                rot[s, 1, lag, rows, :] = (imag * cosine - real * sine).astype(BF16)

    forward(segs)
    forward(1)
    arrived(1, segs)
    start(swaps, segs)
    acc[...] = jnp.zeros_like(acc)
    expand(1)
    arrived_third(segs)
    expand(2)
    arrived(0, segs)
    expand(0)

    def add(slot, s):
        for c in range(2):
            other = (got[slot, s, c].astype(F32) * scale[slot]).astype(BF16)
            mine = rot[s, c].reshape(LAGS * chans, bins)
            acc[slot] += lax.dot_general(
                mine, other, (((1,), (1,)), ((), ())), preferred_element_type=F32
            )

    @pl.loop(0, segs)
    def _(s):
        @pl.when(s + 2 < segs)
        def _():
            forward(s + 2)

        arrived(1, s)
        start(swaps, s)
        add(1, s)
        arrived_third(s)
        add(2, s)
        arrived(0, s)
        add(0, s)

    norm = 1.0 / math.sqrt(segs * bins)
    for slot in range(ROUNDS):
        @pl.loop(0, LAGS * chans // ROWS)
        def _(i):
            rows = pl.ds(pl.multiple_of(i * ROWS, ROWS), ROWS)
            out[slot, rows, :] = (acc[slot, rows, :] * norm).astype(BF16)

    def sent(s):
        for cond, make in own_flows + [relay] + swaps:
            @pl.when(cond)
            def _():
                make(s).wait_send()

    @pl.loop(0, segs)
    def _(s):
        sent(s)

    sent(segs)


def shards(groups, bands, spectra, half_width):
    _, segs, chans, bins = spectra.shape
    inner = lax.axis_index("band") * bins + jnp.arange(bins, dtype=jnp.int32)
    lag_values = jnp.arange(LAGS, dtype=F32) * LAG_STEP
    phases = math.pi * lag_values[:, None] * inner.astype(F32)[None, :] / (bands * bins)
    vmem = pl.BlockSpec(memory_space=pltpu.VMEM)
    pieces = segs + 1
    out = pl.pallas_call(
        functools.partial(kernel, groups, bands),
        out_shape=jax.ShapeDtypeStruct((ROUNDS, LAGS * chans, chans), BF16),
        in_specs=[pl.BlockSpec(memory_space=pl.ANY), vmem, vmem, vmem],
        out_specs=vmem,
        scratch_shapes=[
            pltpu.VMEM((segs, 2, LAGS, chans, bins), BF16),
            pltpu.VMEM((ROUNDS, segs, 2, chans, bins), BF16),
            pltpu.VMEM((ROUNDS, LAGS * chans, chans), F32),
            pltpu.VMEM((ROUNDS + 1, chans // 3, bins), F32),
            pltpu.VMEM((ROUNDS + 1, chans, bins), F32),
            pltpu.VMEM((chans, bins), F32),
            pltpu.VMEM((chans // 3, bins + 2 * LANES), F32),
            pltpu.SemaphoreType.DMA((segs,)),
            pltpu.SemaphoreType.DMA((5, pieces)),
            pltpu.SemaphoreType.DMA((ROUNDS, pieces)),
            pltpu.SemaphoreType.DMA((2,)),
            pltpu.SemaphoreType.DMA((2,)),
        ],
        compiler_params=pltpu.CompilerParams(
            collective_id=0, has_side_effects=True, vmem_limit_bytes=66_500_000
        ),
        cost_estimate=pl.CostEstimate(
            flops=2 * ROUNDS * LAGS * chans * chans * 2 * segs * bins,
            bytes_accessed=2 * spectra.size * 4, transcendentals=0,
        ),
    )(spectra, half_width.reshape(1, bins), jnp.cos(phases), jnp.sin(phases))
    return jnp.transpose(out.reshape(ROUNDS, LAGS, chans, chans), (2, 0, 1, 3))


def solution(mesh):
    in_specs = (P(None, None, "sta", "band"), P("band"))
    out_specs = P("sta", None, "band", None)
    body = functools.partial(shards, mesh.shape["sta"], mesh.shape["band"])
    return jax.shard_map(body, mesh=mesh, in_specs=in_specs, out_specs=out_specs, check_vma=False)
```
